32 devices in a mesh: row: 8 (over z, y), col: 4 (over x, core).
Axes of the slice: x: 2, y: 2, z: 4, core: 2. Of those that a mesh axis runs over, the one named last changes fastest.
Arguments:
- markov: bfloat16 [128, 512, 64], P(('row', 'col')), may hold values from -14 to 14, as said below
- probes: bfloat16 [16, 1024], P(None, 'col'), may hold values from -0.1875 to 0.1875
Outputs:
- range_basis: bfloat16 [16, 65536], P(None, ('row', 'col'))
- projected: float32 [16, 1024], P(None, 'col')
The draws below stay inside these ranges and needn't reach their ends.
Inputs may be any that keep to these rules, and one draw needn't show every extreme that they name: `markov`: markov blocks of a measured response.
All inputs are finite; a program needn't handle non-finite values.
Results may differ from the reference program's by a relative error of at most 0.0049.
Values may be sent and summed in bfloat16 or wider, within the bound.
A program may use at most 64 MiB of HBM per device.

```python
import math
import jax
import jax.numpy as jnp
from jax import lax

SENSORS = 512
ACTUATORS = 64
PROBE_COUNT = 16
BLOCKS_DEV = 4
TILE_ROWS = 16
STEPS = 128
BLOCK_COLS = 16
ROWS = 65536
COLS = 1024
N_COL = 4


def draw_markov(key, part):
    key = jax.random.fold_in(key, 11)
    noise_key, sensor_key = jax.random.split(key)
    entries = jnp.clip(jax.random.normal(noise_key, (STEPS, SENSORS, ACTUATORS), jnp.float32), -4.0, 4.0)
    spread = 10.0
    sensor_gain = jnp.exp(jax.random.uniform(sensor_key, (1, SENSORS, 1), jnp.float32) * jnp.log(spread)) / 3.0
    time_decay = jnp.exp(-2.3 * jnp.arange(STEPS, dtype=jnp.float32)[:, None, None] / STEPS)
    return (entries * sensor_gain * time_decay).astype(jnp.bfloat16)


def levels(rng, extent, shards, low, top_value):
    def one(position, parts):
        draws = jax.random.uniform(jax.random.fold_in(jax.random.fold_in(rng, 6), position), (parts,), jnp.float32, low / len(shards), top_value / len(shards))
        return jnp.repeat(jnp.exp(draws), extent[position] // parts).reshape((-1,) + (1,) * (len(extent) - position - 1))

    loudness = one(*shards[0])
    for cut in shards[1:]:
        loudness = loudness * one(*cut)
    return loudness


def centred(rng, extent, scale, most, cuts=(), kind=jnp.bfloat16):
    array = scale * jax.random.normal(rng, extent, jnp.float32)
    if cuts:
        array = array * levels(rng, extent, cuts, -0.22, 0.18)
    return jnp.clip(array, -most, most).astype(kind)


def setup_inputs(seed: int = 0) -> dict:
    streams_of = jax.random.split(jax.random.key(seed), 3)
    return {
        "markov": draw_markov(jax.random.fold_in(streams_of[2], 71), 0),
        "probes": centred(streams_of[1], (PROBE_COUNT, COLS), COLS ** -0.5, 0.1875, ((1, 4),)),
    }


def reference(markov, probes):
    padded = jnp.concatenate([markov, jnp.zeros((BLOCK_COLS, SENSORS, ACTUATORS), markov.dtype)], 0)
    weights = probes.reshape(PROBE_COUNT, BLOCK_COLS, ACTUATORS)
    row_groups = STEPS // TILE_ROWS
    zero_index = jnp.zeros((), jnp.int32)

    def column_tile(running_sum, tile_index):
        tile_index = tile_index.astype(jnp.int32)

        def row_block(row_index):
            first_row = (row_index * TILE_ROWS).astype(jnp.int32)
            running = jnp.zeros((PROBE_COUNT, TILE_ROWS, SENSORS), jnp.float32)
            for offset in range(BLOCKS_DEV):
                column = (tile_index * BLOCKS_DEV + offset).astype(jnp.int32)
                start_row = (first_row + column).astype(jnp.int32)
                slab_rows = lax.dynamic_slice(padded, (start_row, zero_index, zero_index), (TILE_ROWS, SENSORS, ACTUATORS)).astype(jnp.float32)
                weight_col = lax.dynamic_slice(weights, (zero_index, column, zero_index), (PROBE_COUNT, 1, ACTUATORS))[:, 0].astype(jnp.float32)
                running = running + jnp.einsum('qm,kpm->qkp', weight_col, slab_rows)
            return running
        pieces = lax.map(row_block, jnp.arange(row_groups, dtype=jnp.int32))
        partial_value = jnp.transpose(pieces, (1, 0, 2, 3)).reshape(PROBE_COUNT, ROWS)
        return (running_sum + partial_value, None)
    response, _ = lax.scan(column_tile, jnp.zeros((PROBE_COUNT, ROWS), jnp.float32), jnp.arange(N_COL, dtype=jnp.int32))
    mean_square = lax.optimization_barrier(jnp.sum(response * response, axis=1, keepdims=True)) / ROWS
    range_basis = (response * lax.rsqrt(mean_square + 1e-06)).astype(jnp.bfloat16)
    blocks = range_basis.reshape(PROBE_COUNT, STEPS, SENSORS)

    def project(column):
        column = column.astype(jnp.int32)

        def add_group(running, row_index):
            first_row = (row_index * TILE_ROWS).astype(jnp.int32)
            start_row = (first_row + column).astype(jnp.int32)
            slab_rows = lax.dynamic_slice(padded, (start_row, zero_index, zero_index), (TILE_ROWS, SENSORS, ACTUATORS)).astype(jnp.float32)
            basis_part = lax.dynamic_slice(blocks, (zero_index, first_row, zero_index), (PROBE_COUNT, TILE_ROWS, SENSORS)).astype(jnp.float32)
            return (running + jnp.einsum('qkp,kpm->qm', basis_part, slab_rows), None)
        running, _ = lax.scan(add_group, jnp.zeros((PROBE_COUNT, ACTUATORS), jnp.float32), jnp.arange(row_groups, dtype=jnp.int32))
        return running
    columns = lax.map(project, jnp.arange(BLOCK_COLS, dtype=jnp.int32))
    projected = jnp.transpose(columns, (1, 0, 2)).reshape(PROBE_COUNT, COLS) * (1.0 / math.sqrt(ROWS))
    return (range_basis, projected)
```

```python
import functools
import math

import jax
import jax.numpy as jnp
from jax import lax
from jax.experimental import pallas as pl
from jax.experimental.pallas import tpu as pltpu
from jax.sharding import PartitionSpec as P

MESH = pl.DeviceIdType.MESH
LANES = 128


def body(nr, nc, blocks_dev, markov, probes, basis_out, proj_out,
         pbuf, image_send, image_recv, image, back_send, back_recv,
         tile_acc, tile_send, tile_recv, all_send, all_recv,
         sem_ps, sem_pr, sem_is, sem_ir, sem_bs, sem_br, sem_ts, sem_tr, sem_as, sem_ar):
    f32, bf16 = jnp.float32, jnp.bfloat16
    q, tile = probes.shape
    sensors = markov.shape[1]
    act = tile // blocks_dev
    n = nr * nc
    row, col = lax.axis_index("row"), lax.axis_index("col")
    me = row * nc + col

    def at(d):
        return (d // nc, d % nc)

    def remote(src, dst, send, recv, device):
        return pltpu.make_async_remote_copy(src_ref=src, dst_ref=dst, send_sem=send, recv_sem=recv,
                                            device_id=device, device_id_type=MESH)

    barrier = pltpu.get_barrier_semaphore()

    def greet(device):
        pl.semaphore_signal(barrier, inc=1, device_id=device, device_id_type=MESH)

    for k in range(1, nc):
        greet((row, (col + k) % nc))
    for k in range(nc):
        @pl.when((row > 0) & (k >= col))
        def _():
            greet((row - 1, k))

        @pl.when((row < nr - 1) & (k <= col))
        def _():
            greet((row + 1, k))
    for k in range(nr):
        @pl.when((k > row + 1) | (k < row - 1))
        def _():
            greet((k, col))
    up = (row > 0).astype(jnp.int32)
    down = (row < nr - 1).astype(jnp.int32)
    pl.semaphore_wait(barrier, (nc - 1) + up * (nc - col) + down * (col + 1) + (nr - 1 - up - down))

    for k in range(1, nc):
        remote(probes, pbuf.at[col], sem_ps.at[k], sem_pr.at[col], (row, (col + k) % nc)).start()
    pbuf[col] = probes[...]
    for k in range(nc):
        @pl.when(col != k)
        def _():
            remote(probes, pbuf.at[k], sem_ps.at[0], sem_pr.at[k], (row, k)).wait_recv()

    lane = lax.broadcasted_iota(jnp.int32, (q, tile), 1)
    zero = jnp.zeros((q, tile), f32)
    parts = [pbuf[k].astype(f32) for k in range(nc)]
    rolled = [[p] + [pltpu.roll(p, act * u, 1) for u in range(1, blocks_dev)] for p in parts]

    def weights(t):
        rows = []
        for u in range(blocks_dev):
            upper = rolled[t][u] if t < nc else zero
            lower = rolled[t - 1][u] if t > 0 else zero
            rows.append(upper if u == 0 else jnp.where(lane < act * u, lower, upper))
        return jnp.concatenate(rows, 0).astype(bf16)

    def partial_image(t):
        return jnp.dot(weights(t), markov[...], preferred_element_type=f32)

    def rows_of(t):
        return pl.ds(q, (blocks_dev - 1) * q) if t == nc else pl.ds(0, blocks_dev * q)

    def image_copy(t, device):
        return remote(image_send.at[t - 1, rows_of(t)], image_recv.at[t - 1, rows_of(t)],
                      sem_is.at[t - 1], sem_ir.at[t - 1], device)

    def back_copy(t, device):
        return remote(back_send.at[rows_of(t)], back_recv.at[t - 1, rows_of(t)],
                      sem_bs.at[t - 1], sem_br.at[t - 1], device)

    for t in range(nc, 0, -1):
        @pl.when(me - t >= 0)
        def _():
            image_send[t - 1] = partial_image(t)
            image_copy(t, at(me - t)).start()
    image[...] = partial_image(0)
    for t in range(1, nc + 1):
        @pl.when(me + t < n)
        def _():
            image_copy(t, at(me + t)).wait_recv()
            image[rows_of(t)] += image_recv[t - 1, rows_of(t)]

    back_send[...] = image[...].astype(bf16)
    for t in range(nc, 0, -1):
        @pl.when(me + t < n)
        def _():
            back_copy(t, at(me + t)).start()

    squares = jnp.sum(image[...] * image[...], axis=1, keepdims=True)
    square = squares[0:q]
    for u in range(1, blocks_dev):
        square = square + squares[u * q : (u + 1) * q]
    square = jnp.broadcast_to(square, (q, LANES))
    tile_acc[...] = jnp.zeros_like(tile_acc)

    def project(t, part):
        prod = lax.dot_general(part, markov[...], (((1,), (1,)), ((), ())), preferred_element_type=f32)
        upper, lower = zero, zero
        for u in range(blocks_dev):
            piece = prod[u * q : (u + 1) * q]
            if u == 0:
                upper = upper + piece
                continue
            piece = pltpu.roll(piece, tile - act * u, 1)
            upper = upper + jnp.where(lane < tile - act * u, piece, 0.0)
            lower = lower + jnp.where(lane < tile - act * u, 0.0, piece)
        if t < nc:
            tile_acc[t] += upper
        if t > 0:
            tile_acc[t - 1] += lower

    def tile_copy(k, device):
        return remote(tile_send.at[k], tile_recv.at[col], sem_ts.at[k], sem_tr.at[col], device)

    project(0, back_send[...])
    for t in range(1, nc + 1):
        @pl.when(me - t >= 0)
        def _():
            back_copy(t, at(me - t)).wait_recv()
            part = back_recv[t - 1, rows_of(t)]
            if t == nc:
                part = jnp.concatenate([jnp.zeros((q, sensors), bf16), part], 0)
            project(t, part)
        tile_send[t - 1, :, 0:tile] = tile_acc[t - 1]
        tile_send[t - 1, :, tile : tile + LANES] = square

        @pl.when(col != t - 1)
        def _():
            tile_copy(t - 1, (row, t - 1)).start()

    tile_recv[col] = tile_send[col]
    for k in range(nc):
        @pl.when(col != k)
        def _():
            remote(tile_send.at[k], tile_recv.at[k], sem_ts.at[k], sem_tr.at[k], (row, k)).wait_recv()
    total = tile_recv[0]
    for k in range(1, nc):
        total = total + tile_recv[k]
    all_send[...] = total
    all_recv[row] = total
    for k in range(1, nr):
        remote(all_send, all_recv.at[row], sem_as.at[k], sem_ar.at[row], ((row + k) % nr, col)).start()
    for k in range(nr):
        @pl.when(row != k)
        def _():
            remote(all_send, all_recv.at[k], sem_as.at[0], sem_ar.at[k], (k, col)).wait_recv()
    total = all_recv[0]
    for k in range(1, nr):
        total = total + all_recv[k]

    count = n * blocks_dev * sensors
    scale = lax.rsqrt(total[:, tile : tile + 1] / count + 1e-06)
    proj_out[...] = total[:, 0:tile] * scale * (1.0 / math.sqrt(count))
    for u in range(blocks_dev):
        basis_out[:, u * sensors : (u + 1) * sensors] = (image[u * q : (u + 1) * q] * scale).astype(bf16)

    for k in range(1, nc):
        remote(probes, pbuf.at[col], sem_ps.at[k], sem_pr.at[col], (row, (col + k) % nc)).wait_send()
    for t in range(1, nc + 1):
        @pl.when(me - t >= 0)
        def _():
            image_copy(t, at(me - t)).wait_send()

        @pl.when(me + t < n)
        def _():
            back_copy(t, at(me + t)).wait_send()

        @pl.when(col != t - 1)
        def _():
            tile_copy(t - 1, (row, t - 1)).wait_send()
    for k in range(1, nr):
        remote(all_send, all_recv.at[row], sem_as.at[k], sem_ar.at[row], ((row + k) % nr, col)).wait_send()


def on_device(nr, nc, markov, probes):
    blocks_dev, sensors, act = markov.shape
    q, tile = probes.shape
    flat = jnp.transpose(markov, (0, 2, 1)).reshape(blocks_dev * act, sensors)
    vmem = pl.BlockSpec(memory_space=pltpu.VMEM)
    f32, bf16 = jnp.float32, jnp.bfloat16
    m = blocks_dev * q
    dma = pltpu.SemaphoreType.DMA
    return pl.pallas_call(
        functools.partial(body, nr, nc, blocks_dev),
        out_shape=(jax.ShapeDtypeStruct((q, blocks_dev * sensors), bf16), jax.ShapeDtypeStruct((q, tile), f32)),
        in_specs=[vmem, vmem],
        out_specs=(vmem, vmem),
        scratch_shapes=[
            pltpu.VMEM((nc, q, tile), bf16),
            pltpu.VMEM((nc, m, sensors), f32),
            pltpu.VMEM((nc, m, sensors), f32),
            pltpu.VMEM((m, sensors), f32),
            pltpu.VMEM((m, sensors), bf16),
            pltpu.VMEM((nc, m, sensors), bf16),
            pltpu.VMEM((nc, q, tile), f32),
            pltpu.VMEM((nc, q, tile + LANES), f32),
            pltpu.VMEM((nc, q, tile + LANES), f32),
            pltpu.VMEM((q, tile + LANES), f32),
            pltpu.VMEM((nr, q, tile + LANES), f32),
            dma((nc,)), dma((nc,)), dma((nc,)), dma((nc,)), dma((nc,)), dma((nc,)),
            dma((nc,)), dma((nc,)), dma((nr,)), dma((nr,)),
        ],
        compiler_params=pltpu.CompilerParams(
            collective_id=0, has_side_effects=True, vmem_limit_bytes=32 * 1024 * 1024
        ),
    )(flat, probes)


def solution(mesh):
    return jax.shard_map(
        functools.partial(on_device, mesh.shape["row"], mesh.shape["col"]),
        mesh=mesh,
        in_specs=(P(("row", "col"), None, None), P(None, "col")),
        out_specs=(P(None, ("row", "col")), P(None, "col")),
        check_vma=False,
    )
```

```python
import functools
import math

import jax
import jax.numpy as jnp
from jax import lax
from jax.experimental import pallas as pl
from jax.experimental.pallas import tpu as pltpu
from jax.sharding import PartitionSpec as P

MESH = pl.DeviceIdType.MESH
LANES = 128
CHUNKS = 4


def body(nr, nc, blocks_dev, chunks, markov, probes, basis_out, proj_out,
         window, pbuf, weight, image, tile_acc, tile_send, tile_recv, all_send, all_recv,
         sem_in, sem_ps, sem_pr, sem_own, sem_up, sem_relay, sem_fwd, sem_win,
         sem_ts, sem_tr, sem_as, sem_ar):
    f32, bf16 = jnp.float32, jnp.bfloat16
    q, tile = probes.shape
    sensors = markov.shape[1]
    act = tile // blocks_dev
    n = nr * nc
    pair = 2 if nr % 2 == 0 else 1
    row, col = lax.axis_index("row"), lax.axis_index("col")
    me = row * nc + col
    high, low = row // pair, row % pair
    odd = col % 2
    sibling = (row, col + 1 - 2 * odd)
    sent = []

    load_markov = pltpu.make_async_copy(markov, window.at[0], sem_in.at[0])
    load_probes = pltpu.make_async_copy(probes, pbuf.at[col], sem_in.at[1])
    load_markov.start()
    load_probes.start()

    def remote(src, dst, send, recv, device):
        return pltpu.make_async_remote_copy(src_ref=src, dst_ref=dst, send_sem=send, recv_sem=recv,
                                            device_id=device, device_id_type=MESH)

    def send(cond, copy):
        if cond is None:
            copy().start()
        else:
            @pl.when(cond)
            def _():
                copy().start()
        sent.append((cond, copy))

    barrier = pltpu.get_barrier_semaphore()

    def greet(device):
        pl.semaphore_signal(barrier, inc=1, device_id=device, device_id_type=MESH)

    for k in range(1, nc):
        greet((row, (col + k) % nc))
    if pair == 2:
        for k in range(nc):
            greet((row + 1 - 2 * low, k))
    groups = nr // pair
    for k in range(1, groups):
        greet(((high + k) % groups * pair + low, col))
    if pair == 2:
        step = 2 * low - 1
        lone = ((row + step >= 0) & (row + step < nr)).astype(jnp.int32)

        @pl.when(lone == 1)
        def _():
            greet((row + step, col))
        pl.semaphore_wait(barrier, nc - 1 + nc + groups - 1 + lone)
    else:
        pl.semaphore_wait(barrier, nc - 1 + groups - 1)

    def exists(t):
        return me + t < n

    def rows(v):
        size = blocks_dev * act // chunks
        return pl.ds(v * size, size)

    def win_copy(here, there, v, sem, device):
        return remote(window.at[here, rows(v)], window.at[there, rows(v)], sem, sem_win.at[there, v], device)

    def arrived(t, v):
        win_copy(t, t, v, sem_up.at[0], sibling).wait_recv()

    load_markov.wait()
    for v in range(chunks):
        send(row > 0, functools.partial(win_copy, 0, nc, v, sem_up.at[v], (row - 1, col)))
        for k in range(2, nc, 2):
            send(col >= k, functools.partial(win_copy, 0, k, v, sem_own.at[k, v], (row, col - k)))
    load_probes.wait()
    for k in range(1, nc):
        send(None, functools.partial(remote, pbuf.at[col], pbuf.at[col], sem_ps.at[k], sem_pr.at[col],
                                     (row, (col + k) % nc)))

    def forward(t, v):
        needed = (odd == 0) if t == nc else (odd == 1) if t == 0 else None
        cond = exists(t) if needed is None else exists(t) & needed
        there = t - 1 + 2 * odd
        send(cond, functools.partial(win_copy, t, there, v, sem_fwd.at[t, v], sibling))

    for v in range(chunks):
        forward(0, v)

    for k in range(nc):
        @pl.when(col != k)
        def _():
            remote(pbuf.at[k], pbuf.at[k], sem_ps.at[0], sem_pr.at[k], sibling).wait_recv()
    lane = lax.broadcasted_iota(jnp.int32, (q, tile), 1)
    zero = jnp.zeros((q, tile), f32)
    parts = [pbuf[k].astype(f32) for k in range(nc)]
    rolled = [[p] + [pltpu.roll(p, act * u, 1) for u in range(1, blocks_dev)] for p in parts]
    for t in range(nc + 1):
        for u in range(blocks_dev):
            upper = rolled[t][u] if t < nc else zero
            lower = rolled[t - 1][u] if t > 0 else zero
            part = upper if u == 0 else jnp.where(lane < act * u, lower, upper)
            weight[t, u * q : (u + 1) * q] = part.astype(bf16)

    def add_image(t):
        image[...] += jnp.dot(weight[t], window[t], preferred_element_type=f32)

    image[...] = jnp.dot(weight[0], window[0], preferred_element_type=f32)

    for v in range(chunks):
        @pl.when(exists(nc))
        def _():
            arrived(nc, v)
        for k in range(2, nc, 2):
            send(exists(nc) & (col + k < nc),
                 functools.partial(win_copy, nc, nc - k, v, sem_relay.at[k, v], (row, col + k)))
        forward(nc, v)
        for t in range(2, nc, 2):
            @pl.when(col + t < nc)
            def _():
                arrived(t, v)
                win_copy(t, t - 1 + 2 * odd, v, sem_fwd.at[t, v], sibling).start()

    @pl.when(exists(nc))
    def _():
        add_image(nc)
    for v in range(chunks):
        for t in range(2, nc, 2):
            @pl.when(exists(t) & (col + t >= nc))
            def _():
                arrived(t, v)
                win_copy(t, t - 1 + 2 * odd, v, sem_fwd.at[t, v], sibling).start()
            sent.append((exists(t), functools.partial(
                win_copy, t, t - 1 + 2 * odd, v, sem_fwd.at[t, v], sibling)))
    for t in [*range(2, nc, 2), *range(1, nc, 2)]:
        @pl.when(exists(t))
        def _():
            if t % 2 == 1:
                for v in range(chunks):
                    arrived(t, v)
            add_image(t)

    squares = jnp.sum(image[...] * image[...], axis=1, keepdims=True)
    square = squares[0:q]
    for u in range(1, blocks_dev):
        square = square + squares[u * q : (u + 1) * q]
    square = jnp.broadcast_to(square, (q, LANES))
    tile_acc[...] = jnp.zeros_like(tile_acc)
    image16 = image[...].astype(bf16)

    def project(t):
        prod = lax.dot_general(image16, window[t], (((1,), (1,)), ((), ())), preferred_element_type=f32)
        upper, lower = zero, zero
        for u in range(blocks_dev):
            piece = prod[u * q : (u + 1) * q]
            if u == 0:
                upper = upper + piece
                continue
            piece = pltpu.roll(piece, tile - act * u, 1)
            upper = upper + jnp.where(lane < tile - act * u, piece, 0.0)
            lower = lower + jnp.where(lane < tile - act * u, 0.0, piece)
        if t < nc:
            tile_acc[t] += upper
        if t > 0:
            tile_acc[t - 1] += lower

    def tile_copy(k, r, sem):
        place = low * nc + col
        return remote(tile_send.at[k], tile_recv.at[place], sem, sem_tr.at[place], (r, k))

    project(0)
    for t in range(1, nc + 1):
        @pl.when(exists(t))
        def _():
            project(t)
        tile_send[t - 1, :, 0:tile] = tile_acc[t - 1]
        tile_send[t - 1, :, tile : tile + LANES] = square
        if pair == 2:
            send(None, functools.partial(tile_copy, t - 1, row + 1 - 2 * low, sem_ts.at[1, t - 1]))
        send(col != t - 1, functools.partial(tile_copy, t - 1, row, sem_ts.at[0, t - 1]))
    tile_recv[low * nc + col] = tile_send[col]
    total = None
    for k in range(pair * nc):
        @pl.when(low * nc + col != k)
        def _():
            remote(tile_recv.at[k], tile_recv.at[k], sem_ts.at[0, 0], sem_tr.at[k], sibling).wait_recv()
    total = tile_recv[0]
    for k in range(1, pair * nc):
        total = total + tile_recv[k]
    all_send[...] = total
    all_recv[high] = total
    for k in range(1, groups):
        send(None, functools.partial(remote, all_send, all_recv.at[high], sem_as.at[k], sem_ar.at[high],
                                     ((high + k) % groups * pair + low, col)))
    for k in range(groups):
        @pl.when(high != k)
        def _():
            remote(all_send, all_recv.at[k], sem_as.at[0], sem_ar.at[k], sibling).wait_recv()
    total = all_recv[0]
    for k in range(1, groups):
        total = total + all_recv[k]

    count = n * blocks_dev * sensors
    scale = lax.rsqrt(total[:, tile : tile + 1] / count + 1e-06)
    proj_out[...] = total[:, 0:tile] * scale * (1.0 / math.sqrt(count))
    for u in range(blocks_dev):
        basis_out[:, u * sensors : (u + 1) * sensors] = (image[u * q : (u + 1) * q] * scale).astype(bf16)

    for cond, copy in sent:
        if cond is None:
            copy().wait_send()
        else:
            @pl.when(cond)
            def _():
                copy().wait_send()


def on_device(nr, nc, markov, probes):
    blocks_dev, sensors, act = markov.shape
    q, tile = probes.shape
    flat = jnp.transpose(markov, (0, 2, 1)).reshape(blocks_dev * act, sensors)
    vmem, anywhere = pl.BlockSpec(memory_space=pltpu.VMEM), pl.BlockSpec(memory_space=pl.ANY)
    f32, bf16 = jnp.float32, jnp.bfloat16
    m = blocks_dev * q
    chunks = CHUNKS
    dma = pltpu.SemaphoreType.DMA
    return pl.pallas_call(
        functools.partial(body, nr, nc, blocks_dev, chunks),
        out_shape=(jax.ShapeDtypeStruct((q, blocks_dev * sensors), bf16), jax.ShapeDtypeStruct((q, tile), f32)),
        in_specs=[anywhere, anywhere],
        out_specs=(vmem, vmem),
        scratch_shapes=[
            pltpu.VMEM((nc + 1, blocks_dev * act, sensors), bf16),
            pltpu.VMEM((nc, q, tile), bf16),
            pltpu.VMEM((nc + 1, m, tile), bf16),
            pltpu.VMEM((m, sensors), f32),
            pltpu.VMEM((nc, q, tile), f32),
            pltpu.VMEM((nc, q, tile + LANES), f32),
            pltpu.VMEM((2 * nc, q, tile + LANES), f32),
            pltpu.VMEM((q, tile + LANES), f32),
            pltpu.VMEM((nr, q, tile + LANES), f32),
            dma((2,)), dma((nc,)), dma((nc,)), dma((nc, chunks)), dma((chunks,)), dma((nc, chunks)),
            dma((nc + 1, chunks)), dma((nc + 1, chunks)),
            dma((2, nc)), dma((2 * nc,)), dma((nr,)), dma((nr,)),
        ],
        compiler_params=pltpu.CompilerParams(
            collective_id=0, has_side_effects=True, vmem_limit_bytes=32 * 1024 * 1024
        ),
    )(flat, probes)


def solution(mesh):
    return jax.shard_map(
        functools.partial(on_device, mesh.shape["row"], mesh.shape["col"]),
        mesh=mesh,
        in_specs=(P(("row", "col"), None, None), P(None, "col")),
        out_specs=(P(None, ("row", "col")), P(None, "col")),
        check_vma=False,
    )
```

```python
import functools
import math

import jax
import jax.numpy as jnp
from jax import lax
from jax.experimental import pallas as pl
from jax.experimental.pallas import tpu as pltpu
from jax.sharding import PartitionSpec as P

MESH = pl.DeviceIdType.MESH
LANES = 128
DIRECT = 4


def body(nr, nc, blocks_dev, chunks, markov, probes, basis_out, proj_out,
         window, pbuf, weight, image, tile_acc, tile_send, tile_recv, all_send, all_recv,
         sem_in, sem_ps, sem_pr, sem_own, sem_up, sem_relay, sem_fwd, sem_win,
         sem_ts, sem_tr, sem_as, sem_ar):
    f32, bf16 = jnp.float32, jnp.bfloat16
    q, tile = probes.shape
    sensors = markov.shape[1]
    act = tile // blocks_dev
    n = nr * nc
    pair = 2 if nr % 2 == 0 else 1
    row, col = lax.axis_index("row"), lax.axis_index("col")
    me = row * nc + col
    high, low = row // pair, row % pair
    odd = col % 2
    sibling = (row, col + 1 - 2 * odd)
    sent = []

    load_markov = pltpu.make_async_copy(markov, window.at[0], sem_in.at[0])
    load_probes = pltpu.make_async_copy(probes, pbuf.at[col], sem_in.at[1])
    load_markov.start()
    load_probes.start()

    def remote(src, dst, send, recv, device):
        return pltpu.make_async_remote_copy(src_ref=src, dst_ref=dst, send_sem=send, recv_sem=recv,
                                            device_id=device, device_id_type=MESH)

    def send(cond, copy):
        if cond is None:
            copy().start()
        else:
            @pl.when(cond)
            def _():
                copy().start()
        sent.append((cond, copy))

    barrier = pltpu.get_barrier_semaphore()

    def greet(device):
        pl.semaphore_signal(barrier, inc=1, device_id=device, device_id_type=MESH)

    for k in range(1, nc):
        greet((row, (col + k) % nc))
    if pair == 2:
        for k in range(nc):
            greet((row + 1 - 2 * low, k))
    groups = nr // pair
    for k in range(1, groups):
        greet(((high + k) % groups * pair + low, col))
    if pair == 2:
        step = 2 * low - 1
        lone = ((row + step >= 0) & (row + step < nr)).astype(jnp.int32)

        met = 0
        for k in range(0, nc, 2):
            other = col - step * k
            meets = lone * ((other >= 0) & (other < nc)).astype(jnp.int32)
            met = met + meets

            @pl.when(meets == 1)
            def _():
                greet((row + step, other))
        pl.semaphore_wait(barrier, nc - 1 + nc + groups - 1 + met)
    else:
        pl.semaphore_wait(barrier, nc - 1 + groups - 1)

    def exists(t):
        return me + t < n

    def rows(v):
        size = blocks_dev * act // chunks
        return pl.ds(v * size, size)

    def win_copy(here, there, v, sem, device):
        return remote(window.at[here, rows(v)], window.at[there, rows(v)], sem, sem_win.at[there, v], device)

    def arrived(t, v):
        win_copy(t, t, v, sem_up.at[0], sibling).wait_recv()

    def up_needs(below, v):
        cond = (below > 0) & (below < nr)
        return cond & (col < nc - 1) if v == chunks - 1 else cond

    @pl.when(col == nc - 1)
    def _():
        window[nc, (chunks - 1) * act :] = jnp.zeros((act, sensors), bf16)
    load_markov.wait()
    for v in range(chunks):
        send(up_needs(row, v), functools.partial(win_copy, 0, nc, v, sem_up.at[v], (row - 1, col)))
        if v < DIRECT:
            for k in range(2, nc, 2):
                send((row > 0) & (col + k < nc),
                     functools.partial(win_copy, 0, nc - k, v, sem_relay.at[k, v], (row - 1, col + k)))
        for k in range(2, nc, 2):
            send(col >= k, functools.partial(win_copy, 0, k, v, sem_own.at[k, v], (row, col - k)))
    load_probes.wait()
    for k in range(1, nc):
        send(None, functools.partial(remote, pbuf.at[col], pbuf.at[col], sem_ps.at[k], sem_pr.at[col],
                                     (row, (col + k) % nc)))

    def forward(t, v):
        needed = (odd == 0) if t == nc else (odd == 1) if t == 0 else None
        cond = exists(t) if needed is None else exists(t) & needed
        there = t - 1 + 2 * odd
        send(cond, functools.partial(win_copy, t, there, v, sem_fwd.at[t, v], sibling))

    for v in range(chunks):
        forward(0, v)

    for k in range(nc):
        @pl.when(col != k)
        def _():
            remote(pbuf.at[k], pbuf.at[k], sem_ps.at[0], sem_pr.at[k], sibling).wait_recv()
    lane = lax.broadcasted_iota(jnp.int32, (q, tile), 1)
    zero = jnp.zeros((q, tile), f32)
    parts = [pbuf[k].astype(f32) for k in range(nc)]
    rolled = [[p] + [pltpu.roll(p, act * u, 1) for u in range(1, blocks_dev)] for p in parts]
    for t in range(nc + 1):
        for u in range(blocks_dev):
            upper = rolled[t][u] if t < nc else zero
            lower = rolled[t - 1][u] if t > 0 else zero
            part = upper if u == 0 else jnp.where(lane < act * u, lower, upper)
            weight[t, u * q : (u + 1) * q] = part.astype(bf16)

    def add_image(t):
        image[...] += jnp.dot(weight[t], window[t], preferred_element_type=f32)

    image[...] = jnp.dot(weight[0], window[0], preferred_element_type=f32)

    for v in reversed(range(chunks)):
        @pl.when(up_needs(row + 1, v))
        def _():
            arrived(nc, v)
        for k in range(2, nc, 2) if v >= DIRECT else ():
            send(exists(nc) & (col + k < nc),
                 functools.partial(win_copy, nc, nc - k, v, sem_relay.at[k, v], (row, col + k)))
        forward(nc, v)
        for t in range(2, nc, 2):
            @pl.when(col + t < nc)
            def _():
                arrived(t, v)
                win_copy(t, t - 1 + 2 * odd, v, sem_fwd.at[t, v], sibling).start()

    @pl.when(exists(nc))
    def _():
        add_image(nc)
    for v in range(chunks):
        for t in range(2, nc, 2):
            @pl.when(exists(t) & (col + t >= nc))
            def _():
                arrived(t, v)
                win_copy(t, t - 1 + 2 * odd, v, sem_fwd.at[t, v], sibling).start()
            sent.append((exists(t), functools.partial(
                win_copy, t, t - 1 + 2 * odd, v, sem_fwd.at[t, v], sibling)))
    for t in [*range(2, nc, 2), *range(1, nc, 2)]:
        @pl.when(exists(t))
        def _():
            if t % 2 == 1:
                for v in range(chunks):
                    arrived(t, v)
            add_image(t)

    squares = jnp.sum(image[...] * image[...], axis=1, keepdims=True)
    square = squares[0:q]
    for u in range(1, blocks_dev):
        square = square + squares[u * q : (u + 1) * q]
    square = jnp.broadcast_to(square, (q, LANES))
    tile_acc[...] = jnp.zeros_like(tile_acc)
    image16 = image[...].astype(bf16)

    def project(t):
        prod = lax.dot_general(image16, window[t], (((1,), (1,)), ((), ())), preferred_element_type=f32)
        upper, lower = zero, zero
        for u in range(blocks_dev):
            piece = prod[u * q : (u + 1) * q]
            if u == 0:
                upper = upper + piece
                continue
            piece = pltpu.roll(piece, tile - act * u, 1)
            upper = upper + jnp.where(lane < tile - act * u, piece, 0.0)
            lower = lower + jnp.where(lane < tile - act * u, 0.0, piece)
        if t < nc:
            tile_acc[t] += upper
        if t > 0:
            tile_acc[t - 1] += lower

    def tile_copy(k, r, sem):
        place = low * nc + col
        return remote(tile_send.at[k], tile_recv.at[place], sem, sem_tr.at[place], (r, k))

    project(0)
    for t in range(1, nc + 1):
        @pl.when(exists(t))
        def _():
            project(t)
        tile_send[t - 1, :, 0:tile] = tile_acc[t - 1]
        tile_send[t - 1, :, tile : tile + LANES] = square
        if pair == 2:
            send(None, functools.partial(tile_copy, t - 1, row + 1 - 2 * low, sem_ts.at[1, t - 1]))
        send(col != t - 1, functools.partial(tile_copy, t - 1, row, sem_ts.at[0, t - 1]))
    tile_recv[low * nc + col] = tile_send[col]
    total = None
    for k in range(pair * nc):
        @pl.when(low * nc + col != k)
        def _():
            remote(tile_recv.at[k], tile_recv.at[k], sem_ts.at[0, 0], sem_tr.at[k], sibling).wait_recv()
    total = tile_recv[0]
    for k in range(1, pair * nc):
        total = total + tile_recv[k]
    all_send[...] = total
    all_recv[high] = total
    for k in range(1, groups):
        send(None, functools.partial(remote, all_send, all_recv.at[high], sem_as.at[k], sem_ar.at[high],
                                     ((high + k) % groups * pair + low, col)))
    for k in range(groups):
        @pl.when(high != k)
        def _():
            remote(all_send, all_recv.at[k], sem_as.at[0], sem_ar.at[k], sibling).wait_recv()
    total = all_recv[0]
    for k in range(1, groups):
        total = total + all_recv[k]

    count = n * blocks_dev * sensors
    scale = lax.rsqrt(total[:, tile : tile + 1] / count + 1e-06)
    proj_out[...] = total[:, 0:tile] * scale * (1.0 / math.sqrt(count))
    for u in range(blocks_dev):
        basis_out[:, u * sensors : (u + 1) * sensors] = (image[u * q : (u + 1) * q] * scale).astype(bf16)

    for cond, copy in sent:
        if cond is None:
            copy().wait_send()
        else:
            @pl.when(cond)
            def _():
                copy().wait_send()


def on_device(nr, nc, markov, probes):
    blocks_dev, sensors, act = markov.shape
    q, tile = probes.shape
    flat = jnp.transpose(markov, (0, 2, 1)).reshape(blocks_dev * act, sensors)
    vmem, anywhere = pl.BlockSpec(memory_space=pltpu.VMEM), pl.BlockSpec(memory_space=pl.ANY)
    f32, bf16 = jnp.float32, jnp.bfloat16
    m = blocks_dev * q
    chunks = blocks_dev
    dma = pltpu.SemaphoreType.DMA
    return pl.pallas_call(
        functools.partial(body, nr, nc, blocks_dev, chunks),
        out_shape=(jax.ShapeDtypeStruct((q, blocks_dev * sensors), bf16), jax.ShapeDtypeStruct((q, tile), f32)),
        in_specs=[anywhere, anywhere],
        out_specs=(vmem, vmem),
        scratch_shapes=[
            pltpu.VMEM((nc + 1, blocks_dev * act, sensors), bf16),
            pltpu.VMEM((nc, q, tile), bf16),
            pltpu.VMEM((nc + 1, m, tile), bf16),
            pltpu.VMEM((m, sensors), f32),
            pltpu.VMEM((nc, q, tile), f32),
            pltpu.VMEM((nc, q, tile + LANES), f32),
            pltpu.VMEM((2 * nc, q, tile + LANES), f32),
            pltpu.VMEM((q, tile + LANES), f32),
            pltpu.VMEM((nr, q, tile + LANES), f32),
            dma((2,)), dma((nc,)), dma((nc,)), dma((nc, chunks)), dma((chunks,)), dma((nc, chunks)),
            dma((nc + 1, chunks)), dma((nc + 1, chunks)),
            dma((2, nc)), dma((2 * nc,)), dma((nr,)), dma((nr,)),
        ],
        compiler_params=pltpu.CompilerParams(
            collective_id=0, has_side_effects=True, vmem_limit_bytes=32 * 1024 * 1024
        ),
    )(flat, probes)


def solution(mesh):
    return jax.shard_map(
        functools.partial(on_device, mesh.shape["row"], mesh.shape["col"]),
        mesh=mesh,
        in_specs=(P(("row", "col"), None, None), P(None, "col")),
        out_specs=(P(None, ("row", "col")), P(None, "col")),
        check_vma=False,
    )
```

```python
import functools
import math

import jax
import jax.numpy as jnp
from jax import lax
from jax.experimental import pallas as pl
from jax.experimental.pallas import tpu as pltpu
from jax.sharding import PartitionSpec as P

MESH = pl.DeviceIdType.MESH
LANES = 128
DIRECT = 3


def body(nr, nc, blocks_dev, chunks, markov, probes, basis_out, proj_out,
         window, through, sem_ths, sem_thr, pbuf, weight, image, tile_acc, tile_send, tile_recv, all_send, all_recv,
         sem_in, sem_ps, sem_pr, sem_own, sem_up, sem_relay, sem_fwd, sem_win,
         sem_ts, sem_tr, sem_as, sem_ar):
    f32, bf16 = jnp.float32, jnp.bfloat16
    q, tile = probes.shape
    sensors = markov.shape[1]
    act = tile // blocks_dev
    n = nr * nc
    pair = 2 if nr % 2 == 0 else 1
    row, col = lax.axis_index("row"), lax.axis_index("col")
    me = row * nc + col
    high, low = row // pair, row % pair
    odd = col % 2
    sibling = (row, col + 1 - 2 * odd)
    sent = []

    load_markov = pltpu.make_async_copy(markov, window.at[0], sem_in.at[0])
    load_probes = pltpu.make_async_copy(probes, pbuf.at[col], sem_in.at[1])
    load_markov.start()
    load_probes.start()

    def remote(src, dst, send, recv, device):
        return pltpu.make_async_remote_copy(src_ref=src, dst_ref=dst, send_sem=send, recv_sem=recv,
                                            device_id=device, device_id_type=MESH)

    def send(cond, copy):
        if cond is None:
            copy().start()
        else:
            @pl.when(cond)
            def _():
                copy().start()
        sent.append((cond, copy))

    barrier = pltpu.get_barrier_semaphore()

    def greet(device):
        pl.semaphore_signal(barrier, inc=1, device_id=device, device_id_type=MESH)

    for k in range(1, nc):
        greet((row, (col + k) % nc))
    if pair == 2:
        for k in range(nc):
            greet((row + 1 - 2 * low, k))
    groups = nr // pair
    for k in range(1, groups):
        greet(((high + k) % groups * pair + low, col))
    if pair == 2:
        step = 2 * low - 1
        lone = ((row + step >= 0) & (row + step < nr)).astype(jnp.int32)

        met = 0
        for k in range(0, nc, 2):
            other = col - step * k
            meets = lone * ((other >= 0) & (other < nc)).astype(jnp.int32)
            met = met + meets

            @pl.when(meets == 1)
            def _():
                greet((row + step, other))
        pl.semaphore_wait(barrier, nc - 1 + nc + groups - 1 + met)
    else:
        pl.semaphore_wait(barrier, nc - 1 + groups - 1)

    def exists(t):
        return me + t < n

    def rows(v):
        size = blocks_dev * act // chunks
        return pl.ds(v * size, size)

    def win_copy(here, there, v, sem, device):
        return remote(window.at[here, rows(v)], window.at[there, rows(v)], sem, sem_win.at[there, v], device)

    def arrived(t, v):
        win_copy(t, t, v, sem_up.at[0], sibling).wait_recv()

    def up_needs(below, v):
        cond = (below > 0) & (below < nr)
        return cond & (col < nc - 1) if v == chunks - 1 else cond

    @pl.when(col == nc - 1)
    def _():
        window[nc, (chunks - 1) * act :] = jnp.zeros((act, sensors), bf16)
    def through_copy(k, v, device):
        return remote(window.at[0, rows(v)], through.at[k, rows(v)], sem_ths.at[k, v], sem_thr.at[k, v], device)

    def relay_copy(k, v):
        return remote(through.at[k, rows(v)], window.at[nc - k, rows(v)], sem_relay.at[k, v],
                      sem_win.at[nc - k, v], (row - 1, col))

    load_markov.wait()
    for v in range(DIRECT, chunks):
        for k in range(2, nc, 2):
            send((row > 0) & (col + k < nc), functools.partial(through_copy, k, v, (row, col + k)))
    for v in range(chunks):
        send(up_needs(row, v), functools.partial(win_copy, 0, nc, v, sem_up.at[v], (row - 1, col)))
        if v < DIRECT:
            for k in range(2, nc, 2):
                send((row > 0) & (col + k < nc),
                     functools.partial(win_copy, 0, nc - k, v, sem_relay.at[k, v], (row - 1, col + k)))
        for k in range(2, nc, 2):
            send(col >= k, functools.partial(win_copy, 0, k, v, sem_own.at[k, v], (row, col - k)))
    load_probes.wait()
    for k in range(1, nc):
        send(None, functools.partial(remote, pbuf.at[col], pbuf.at[col], sem_ps.at[k], sem_pr.at[col],
                                     (row, (col + k) % nc)))

    def forward(t, v):
        needed = (odd == 0) if t == nc else (odd == 1) if t == 0 else None
        cond = exists(t) if needed is None else exists(t) & needed
        there = t - 1 + 2 * odd
        send(cond, functools.partial(win_copy, t, there, v, sem_fwd.at[t, v], sibling))

    for v in range(chunks):
        forward(0, v)

    for k in range(nc):
        @pl.when(col != k)
        def _():
            remote(pbuf.at[k], pbuf.at[k], sem_ps.at[0], sem_pr.at[k], sibling).wait_recv()
    lane = lax.broadcasted_iota(jnp.int32, (q, tile), 1)
    zero = jnp.zeros((q, tile), f32)
    parts = [pbuf[k].astype(f32) for k in range(nc)]
    rolled = [[p] + [pltpu.roll(p, act * u, 1) for u in range(1, blocks_dev)] for p in parts]
    for t in range(nc + 1):
        for u in range(blocks_dev):
            upper = rolled[t][u] if t < nc else zero
            lower = rolled[t - 1][u] if t > 0 else zero
            part = upper if u == 0 else jnp.where(lane < act * u, lower, upper)
            weight[t, u * q : (u + 1) * q] = part.astype(bf16)

    def add_image(t):
        image[...] += jnp.dot(weight[t], window[t], preferred_element_type=f32)

    image[...] = jnp.dot(weight[0], window[0], preferred_element_type=f32)

    for v in range(DIRECT, chunks):
        for k in range(2, nc, 2):
            @pl.when((row > 0) & (col >= k))
            def _():
                through_copy(k, v, sibling).wait_recv()
                relay_copy(k, v).start()
            sent.append(((row > 0) & (col >= k), functools.partial(relay_copy, k, v)))

    for v in reversed(range(chunks)):
        @pl.when(up_needs(row + 1, v))
        def _():
            arrived(nc, v)
        forward(nc, v)
        for t in range(2, nc, 2):
            @pl.when(col + t < nc)
            def _():
                arrived(t, v)
                win_copy(t, t - 1 + 2 * odd, v, sem_fwd.at[t, v], sibling).start()

    @pl.when(exists(nc))
    def _():
        add_image(nc)
    for v in range(chunks):
        for t in range(2, nc, 2):
            @pl.when(exists(t) & (col + t >= nc))
            def _():
                arrived(t, v)
                win_copy(t, t - 1 + 2 * odd, v, sem_fwd.at[t, v], sibling).start()
            sent.append((exists(t), functools.partial(
                win_copy, t, t - 1 + 2 * odd, v, sem_fwd.at[t, v], sibling)))
    for t in [*range(2, nc, 2), *range(1, nc, 2)]:
        @pl.when(exists(t))
        def _():
            if t % 2 == 1:
                for v in range(chunks):
                    arrived(t, v)
            add_image(t)

    squares = jnp.sum(image[...] * image[...], axis=1, keepdims=True)
    square = squares[0:q]
    for u in range(1, blocks_dev):
        square = square + squares[u * q : (u + 1) * q]
    square = jnp.broadcast_to(square, (q, LANES))
    tile_acc[...] = jnp.zeros_like(tile_acc)
    image16 = image[...].astype(bf16)

    def project(t):
        prod = lax.dot_general(image16, window[t], (((1,), (1,)), ((), ())), preferred_element_type=f32)
        upper, lower = zero, zero
        for u in range(blocks_dev):
            piece = prod[u * q : (u + 1) * q]
            if u == 0:
                upper = upper + piece
                continue
            piece = pltpu.roll(piece, tile - act * u, 1)
            upper = upper + jnp.where(lane < tile - act * u, piece, 0.0)
            lower = lower + jnp.where(lane < tile - act * u, 0.0, piece)
        if t < nc:
            tile_acc[t] += upper
        if t > 0:
            tile_acc[t - 1] += lower

    def tile_copy(k, r, sem):
        place = low * nc + col
        return remote(tile_send.at[k], tile_recv.at[place], sem, sem_tr.at[place], (r, k))

    project(0)
    for t in range(1, nc + 1):
        @pl.when(exists(t))
        def _():
            project(t)
        tile_send[t - 1, :, 0:tile] = tile_acc[t - 1]
        tile_send[t - 1, :, tile : tile + LANES] = square
        if pair == 2:
            send(None, functools.partial(tile_copy, t - 1, row + 1 - 2 * low, sem_ts.at[1, t - 1]))
        send(col != t - 1, functools.partial(tile_copy, t - 1, row, sem_ts.at[0, t - 1]))
    tile_recv[low * nc + col] = tile_send[col]
    total = None
    for k in range(pair * nc):
        @pl.when(low * nc + col != k)
        def _():
            remote(tile_recv.at[k], tile_recv.at[k], sem_ts.at[0, 0], sem_tr.at[k], sibling).wait_recv()
    total = tile_recv[0]
    for k in range(1, pair * nc):
        total = total + tile_recv[k]
    all_send[...] = total
    all_recv[high] = total
    for k in range(1, groups):
        send(None, functools.partial(remote, all_send, all_recv.at[high], sem_as.at[k], sem_ar.at[high],
                                     ((high + k) % groups * pair + low, col)))
    for k in range(groups):
        @pl.when(high != k)
        def _():
            remote(all_send, all_recv.at[k], sem_as.at[0], sem_ar.at[k], sibling).wait_recv()
    total = all_recv[0]
    for k in range(1, groups):
        total = total + all_recv[k]

    count = n * blocks_dev * sensors
    scale = lax.rsqrt(total[:, tile : tile + 1] / count + 1e-06)
    proj_out[...] = total[:, 0:tile] * scale * (1.0 / math.sqrt(count))
    for u in range(blocks_dev):
        basis_out[:, u * sensors : (u + 1) * sensors] = (image[u * q : (u + 1) * q] * scale).astype(bf16)

    for cond, copy in sent:
        if cond is None:
            copy().wait_send()
        else:
            @pl.when(cond)
            def _():
                copy().wait_send()


def on_device(nr, nc, markov, probes):
    blocks_dev, sensors, act = markov.shape
    q, tile = probes.shape
    flat = jnp.transpose(markov, (0, 2, 1)).reshape(blocks_dev * act, sensors)
    vmem, anywhere = pl.BlockSpec(memory_space=pltpu.VMEM), pl.BlockSpec(memory_space=pl.ANY)
    f32, bf16 = jnp.float32, jnp.bfloat16
    m = blocks_dev * q
    chunks = blocks_dev
    dma = pltpu.SemaphoreType.DMA
    return pl.pallas_call(
        functools.partial(body, nr, nc, blocks_dev, chunks),
        out_shape=(jax.ShapeDtypeStruct((q, blocks_dev * sensors), bf16), jax.ShapeDtypeStruct((q, tile), f32)),
        in_specs=[anywhere, anywhere],
        out_specs=(vmem, vmem),
        scratch_shapes=[
            pltpu.VMEM((nc + 1, blocks_dev * act, sensors), bf16),
            pltpu.VMEM((nc, blocks_dev * act, sensors), bf16),
            dma((nc, chunks)), dma((nc, chunks)),
            pltpu.VMEM((nc, q, tile), bf16),
            pltpu.VMEM((nc + 1, m, tile), bf16),
            pltpu.VMEM((m, sensors), f32),
            pltpu.VMEM((nc, q, tile), f32),
            pltpu.VMEM((nc, q, tile + LANES), f32),
            pltpu.VMEM((2 * nc, q, tile + LANES), f32),
            pltpu.VMEM((q, tile + LANES), f32),
            pltpu.VMEM((nr, q, tile + LANES), f32),
            dma((2,)), dma((nc,)), dma((nc,)), dma((nc, chunks)), dma((chunks,)), dma((nc, chunks)),
            dma((nc + 1, chunks)), dma((nc + 1, chunks)),
            dma((2, nc)), dma((2 * nc,)), dma((nr,)), dma((nr,)),
        ],
        compiler_params=pltpu.CompilerParams(
            collective_id=0, has_side_effects=True, vmem_limit_bytes=32 * 1024 * 1024
        ),
    )(flat, probes)


def solution(mesh):
    return jax.shard_map(
        functools.partial(on_device, mesh.shape["row"], mesh.shape["col"]),
        mesh=mesh,
        in_specs=(P(("row", "col"), None, None), P(None, "col")),
        out_specs=(P(None, ("row", "col")), P(None, "col")),
        check_vma=False,
    )
```

```python
import functools
import math

import jax
import jax.numpy as jnp
from jax import lax
from jax.experimental import pallas as pl
from jax.experimental.pallas import tpu as pltpu
from jax.sharding import PartitionSpec as P

MESH = pl.DeviceIdType.MESH
LANES = 128
DIRECT = 3


def body(nr, nc, blocks_dev, chunks, markov, probes, basis_out, proj_out,
         window, through, sem_ths, sem_thr, pbuf, weight, image, tile_acc, tile_send, tile_recv, all_send, all_recv,
         sem_in, sem_ps, sem_pr, sem_own, sem_up, sem_relay, sem_fwd, sem_win,
         sem_ts, sem_tr, sem_as, sem_ar):
    f32, bf16 = jnp.float32, jnp.bfloat16
    q, tile = probes.shape
    sensors = markov.shape[1]
    act = tile // blocks_dev
    n = nr * nc
    pair = 2 if nr % 2 == 0 else 1
    row, col = lax.axis_index("row"), lax.axis_index("col")
    me = row * nc + col
    high, low = row // pair, row % pair
    odd = col % 2
    sibling = (row, col + 1 - 2 * odd)
    sent = []

    load_markov = pltpu.make_async_copy(markov, window.at[0], sem_in.at[0])
    load_probes = pltpu.make_async_copy(probes, pbuf.at[col], sem_in.at[1])
    load_markov.start()
    load_probes.start()

    def remote(src, dst, send, recv, device):
        return pltpu.make_async_remote_copy(src_ref=src, dst_ref=dst, send_sem=send, recv_sem=recv,
                                            device_id=device, device_id_type=MESH)

    def send(cond, copy):
        if cond is None:
            copy().start()
        else:
            @pl.when(cond)
            def _():
                copy().start()
        sent.append((cond, copy))

    barrier = pltpu.get_barrier_semaphore()

    def greet(device):
        pl.semaphore_signal(barrier, inc=1, device_id=device, device_id_type=MESH)

    groups = nr // pair
    for k in range(1, groups):
        greet(((high + k) % groups * pair + low, col))
    if pair == 2:
        for k in range(nc):
            greet((row + 1 - 2 * low, k))
    for k in range(1, nc):
        greet((row, (col + k) % nc))
    if pair == 2:
        step = 2 * low - 1
        lone = ((row + step >= 0) & (row + step < nr)).astype(jnp.int32)

        met = 0
        for k in range(0, nc, 2):
            other = col - step * k
            meets = lone * ((other >= 0) & (other < nc)).astype(jnp.int32)
            met = met + meets

            @pl.when(meets == 1)
            def _():
                greet((row + step, other))
        pl.semaphore_wait(barrier, nc - 1 + nc + groups - 1 + met)
    else:
        pl.semaphore_wait(barrier, nc - 1 + groups - 1)

    def exists(t):
        return me + t < n

    def rows(v):
        size = blocks_dev * act // chunks
        return pl.ds(v * size, size)

    def win_copy(here, there, v, sem, device):
        return remote(window.at[here, rows(v)], window.at[there, rows(v)], sem, sem_win.at[there, v], device)

    def arrived(t, v):
        win_copy(t, t, v, sem_up.at[0], sibling).wait_recv()

    def up_needs(below, v):
        cond = (below > 0) & (below < nr)
        return cond & (col < nc - 1) if v == chunks - 1 else cond

    @pl.when(col == nc - 1)
    def _():
        window[nc, (chunks - 1) * act :] = jnp.zeros((act, sensors), bf16)
    def through_copy(k, v, device):
        return remote(window.at[0, rows(v)], through.at[k, rows(v)], sem_ths.at[k, v], sem_thr.at[k, v], device)

    def relay_copy(k, v):
        return remote(through.at[k, rows(v)], window.at[nc - k, rows(v)], sem_relay.at[k, v],
                      sem_win.at[nc - k, v], (row - 1, col))

    load_markov.wait()
    for v in range(DIRECT, chunks):
        for k in range(2, nc, 2):
            send((row > 0) & (col + k < nc), functools.partial(through_copy, k, v, (row, col + k)))
    for v in range(chunks):
        send(up_needs(row, v), functools.partial(win_copy, 0, nc, v, sem_up.at[v], (row - 1, col)))
        if v < DIRECT:
            for k in range(2, nc, 2):
                send((row > 0) & (col + k < nc),
                     functools.partial(win_copy, 0, nc - k, v, sem_relay.at[k, v], (row - 1, col + k)))
        for k in range(2, nc, 2):
            send(col >= k, functools.partial(win_copy, 0, k, v, sem_own.at[k, v], (row, col - k)))
    load_probes.wait()
    for k in range(1, nc):
        send(None, functools.partial(remote, pbuf.at[col], pbuf.at[col], sem_ps.at[k], sem_pr.at[col],
                                     (row, (col + k) % nc)))

    def forward(t, v):
        needed = (odd == 0) if t == nc else (odd == 1) if t == 0 else None
        cond = exists(t) if needed is None else exists(t) & needed
        there = t - 1 + 2 * odd
        send(cond, functools.partial(win_copy, t, there, v, sem_fwd.at[t, v], sibling))

    for v in range(chunks):
        forward(0, v)

    for k in range(nc):
        @pl.when(col != k)
        def _():
            remote(pbuf.at[k], pbuf.at[k], sem_ps.at[0], sem_pr.at[k], sibling).wait_recv()
    lane = lax.broadcasted_iota(jnp.int32, (q, tile), 1)
    zero = jnp.zeros((q, tile), f32)
    parts = [pbuf[k].astype(f32) for k in range(nc)]
    rolled = [[p] + [pltpu.roll(p, act * u, 1) for u in range(1, blocks_dev)] for p in parts]
    for t in range(nc + 1):
        for u in range(blocks_dev):
            upper = rolled[t][u] if t < nc else zero
            lower = rolled[t - 1][u] if t > 0 else zero
            part = upper if u == 0 else jnp.where(lane < act * u, lower, upper)
            weight[t, u * q : (u + 1) * q] = part.astype(bf16)

    def add_image(t):
        image[...] += jnp.dot(weight[t], window[t], preferred_element_type=f32)

    image[...] = jnp.dot(weight[0], window[0], preferred_element_type=f32)

    for v in range(DIRECT, chunks):
        for k in range(2, nc, 2):
            @pl.when((row > 0) & (col >= k))
            def _():
                through_copy(k, v, sibling).wait_recv()
                relay_copy(k, v).start()
            sent.append(((row > 0) & (col >= k), functools.partial(relay_copy, k, v)))

    for v in reversed(range(chunks)):
        @pl.when(up_needs(row + 1, v))
        def _():
            arrived(nc, v)
        forward(nc, v)
        for t in range(2, nc, 2):
            @pl.when(col + t < nc)
            def _():
                arrived(t, v)
                win_copy(t, t - 1 + 2 * odd, v, sem_fwd.at[t, v], sibling).start()

    @pl.when(exists(nc))
    def _():
        add_image(nc)
    for v in range(chunks):
        for t in range(2, nc, 2):
            @pl.when(exists(t) & (col + t >= nc))
            def _():
                arrived(t, v)
                win_copy(t, t - 1 + 2 * odd, v, sem_fwd.at[t, v], sibling).start()
            sent.append((exists(t), functools.partial(
                win_copy, t, t - 1 + 2 * odd, v, sem_fwd.at[t, v], sibling)))
    for t in [*range(2, nc, 2), *range(1, nc, 2)]:
        @pl.when(exists(t))
        def _():
            if t % 2 == 1:
                for v in range(chunks):
                    arrived(t, v)
            add_image(t)

    squares = jnp.sum(image[...] * image[...], axis=1, keepdims=True)
    square = squares[0:q]
    for u in range(1, blocks_dev):
        square = square + squares[u * q : (u + 1) * q]
    square = jnp.broadcast_to(square, (q, LANES))
    tile_acc[...] = jnp.zeros_like(tile_acc)
    image16 = image[...].astype(bf16)

    def project(t):
        prod = lax.dot_general(image16, window[t], (((1,), (1,)), ((), ())), preferred_element_type=f32)
        upper, lower = zero, zero
        for u in range(blocks_dev):
            piece = prod[u * q : (u + 1) * q]
            if u == 0:
                upper = upper + piece
                continue
            piece = pltpu.roll(piece, tile - act * u, 1)
            upper = upper + jnp.where(lane < tile - act * u, piece, 0.0)
            lower = lower + jnp.where(lane < tile - act * u, 0.0, piece)
        if t < nc:
            tile_acc[t] += upper
        if t > 0:
            tile_acc[t - 1] += lower

    def tile_copy(k, r, sem):
        place = low * nc + col
        return remote(tile_send.at[k], tile_recv.at[place], sem, sem_tr.at[place], (r, k))

    project(0)
    for t in range(1, nc + 1):
        @pl.when(exists(t))
        def _():
            project(t)
        tile_send[t - 1, :, 0:tile] = tile_acc[t - 1]
        tile_send[t - 1, :, tile : tile + LANES] = square
        if pair == 2:
            send(None, functools.partial(tile_copy, t - 1, row + 1 - 2 * low, sem_ts.at[1, t - 1]))
        send(col != t - 1, functools.partial(tile_copy, t - 1, row, sem_ts.at[0, t - 1]))
    tile_recv[low * nc + col] = tile_send[col]
    total = None
    for k in range(pair * nc):
        @pl.when(low * nc + col != k)
        def _():
            remote(tile_recv.at[k], tile_recv.at[k], sem_ts.at[0, 0], sem_tr.at[k], sibling).wait_recv()
    total = tile_recv[0]
    for k in range(1, pair * nc):
        total = total + tile_recv[k]
    all_send[...] = total
    all_recv[high] = total
    for k in range(1, groups):
        send(None, functools.partial(remote, all_send, all_recv.at[high], sem_as.at[k], sem_ar.at[high],
                                     ((high + k) % groups * pair + low, col)))
    for k in range(groups):
        @pl.when(high != k)
        def _():
            remote(all_send, all_recv.at[k], sem_as.at[0], sem_ar.at[k], sibling).wait_recv()
    total = all_recv[0]
    for k in range(1, groups):
        total = total + all_recv[k]

    count = n * blocks_dev * sensors
    scale = lax.rsqrt(total[:, tile : tile + 1] / count + 1e-06)
    proj_out[...] = total[:, 0:tile] * scale * (1.0 / math.sqrt(count))
    for u in range(blocks_dev):
        basis_out[:, u * sensors : (u + 1) * sensors] = (image[u * q : (u + 1) * q] * scale).astype(bf16)

    for cond, copy in sent:
        if cond is None:
            copy().wait_send()
        else:
            @pl.when(cond)
            def _():
                copy().wait_send()


def on_device(nr, nc, markov, probes):
    blocks_dev, sensors, act = markov.shape
    q, tile = probes.shape
    flat = jnp.transpose(markov, (0, 2, 1)).reshape(blocks_dev * act, sensors)
    vmem, anywhere = pl.BlockSpec(memory_space=pltpu.VMEM), pl.BlockSpec(memory_space=pl.ANY)
    f32, bf16 = jnp.float32, jnp.bfloat16
    m = blocks_dev * q
    chunks = blocks_dev
    dma = pltpu.SemaphoreType.DMA
    return pl.pallas_call(
        functools.partial(body, nr, nc, blocks_dev, chunks),
        out_shape=(jax.ShapeDtypeStruct((q, blocks_dev * sensors), bf16), jax.ShapeDtypeStruct((q, tile), f32)),
        in_specs=[anywhere, anywhere],
        out_specs=(vmem, vmem),
        scratch_shapes=[
            pltpu.VMEM((nc + 1, blocks_dev * act, sensors), bf16),
            pltpu.VMEM((nc, blocks_dev * act, sensors), bf16),
            dma((nc, chunks)), dma((nc, chunks)),
            pltpu.VMEM((nc, q, tile), bf16),
            pltpu.VMEM((nc + 1, m, tile), bf16),
            pltpu.VMEM((m, sensors), f32),
            pltpu.VMEM((nc, q, tile), f32),
            pltpu.VMEM((nc, q, tile + LANES), f32),
            pltpu.VMEM((2 * nc, q, tile + LANES), f32),
            pltpu.VMEM((q, tile + LANES), f32),
            pltpu.VMEM((nr, q, tile + LANES), f32),
            dma((2,)), dma((nc,)), dma((nc,)), dma((nc, chunks)), dma((chunks,)), dma((nc, chunks)),
            dma((nc + 1, chunks)), dma((nc + 1, chunks)),
            dma((2, nc)), dma((2 * nc,)), dma((nr,)), dma((nr,)),
        ],
        compiler_params=pltpu.CompilerParams(
            collective_id=0, has_side_effects=True, vmem_limit_bytes=32 * 1024 * 1024
        ),
    )(flat, probes)


def solution(mesh):
    return jax.shard_map(
        functools.partial(on_device, mesh.shape["row"], mesh.shape["col"]),
        mesh=mesh,
        in_specs=(P(("row", "col"), None, None), P(None, "col")),
        out_specs=(P(None, ("row", "col")), P(None, "col")),
        check_vma=False,
    )
```
